512 devices in a mesh: seq: 16 (over z), row: 32 (over y, x, core).
Axes of the slice: x: 4, y: 4, z: 16, core: 2. Of those that a mesh axis runs over, the one named last changes fastest.
Arguments:
- queries: bfloat16 [3, 512, 8192], P(None, 'row'), may hold values from -128 to 128
- prefix_keys: bfloat16 [24576, 512], P('seq'), may hold values from -6 to 6
- prefix_values: bfloat16 [24576, 512], P('seq'), may hold values from -6 to 6
- suffix_keys: bfloat16 [512, 1024, 512], P('row', 'seq'), may hold values from -6 to 6
- suffix_values: bfloat16 [512, 1024, 512], P('row', 'seq'), may hold values from -6 to 6
- new_keys: bfloat16 [3, 512, 512], P(None, 'row'), may hold values from -6 to 6
- new_values: bfloat16 [3, 512, 512], P(None, 'row'), may hold values from -6 to 6
- lengths: int32 [512], P('row'), may hold values from 64 to 1024
- pair_of: int32 [512], replicated, may hold values from 0 to 511, as said below
- guidance: float32 [64], replicated, may hold values from 1 to 3
Outputs:
- guided: bfloat16 [3, 512, 8192], P(None, 'row', 'seq')
The draws below stay inside these ranges and needn't reach their ends.
Inputs may be any that keep to these rules, and one draw needn't show every extreme that they name: pair_of[pair_of[r]] = r; a row of the first half of the 512 rows is paired with a row of the second half, and pair_of[r] // 16 = (r // 16 + 512 / 32) mod (32).
All inputs are finite; a program needn't handle non-finite values.
Results may differ from the reference program's by a relative error of at most 0.014.
Values may be sent and summed in bfloat16 or wider, within the bound.
A program may use at most 128 MiB of HBM per device.

```python
import jax
import jax.numpy as jnp
from jax import lax

H = 64
KVH = 4
HD = 128
STEPS = 3
ROW_DEV = 16
ROWS = 512
PREFIX = 24576
SUF = 1024


def draw_queries(key, part):
    base = jnp.clip(jax.random.normal(key, (STEPS, ROWS, H * HD), jnp.float32), -6.0, 6.0)
    return base.astype(jnp.bfloat16)


def draw_pair_of(key, part):
    half = ROWS // 2
    blocks = half // ROW_DEV
    scores = jax.random.randint(jax.random.fold_in(key, 7), (blocks, ROW_DEV), 0, 1 << 20).astype(jnp.int32)
    scores = scores * ROW_DEV + jnp.arange(ROW_DEV, dtype=jnp.int32)[None, :]
    order = jnp.argsort(scores, axis=-1, stable=True).astype(jnp.int32)
    base = half + jnp.arange(blocks, dtype=jnp.int32)[:, None] * ROW_DEV
    upper = (base + order).reshape(half)
    lower = jnp.arange(half, dtype=jnp.int32)
    paired = jnp.zeros((ROWS,), jnp.int32).at[lower].set(upper).at[upper].set(lower)
    return paired


def with_ends(values, own_key, low, largest):
    place = [jax.random.randint(jax.random.fold_in(own_key, axis), (), 0, length) for axis, length in enumerate(values.shape)]
    main_axis = values.shape.index(max(values.shape))
    neighbour = place[:main_axis] + [(place[main_axis] + 1) % values.shape[main_axis]] + place[main_axis + 1:]
    return values.at[tuple(place)].set(low).at[tuple(neighbour)].set(largest)


def block_levels(stream_key, shape, pieces, least, high):
    def one(position, parts):
        steps = jax.random.uniform(jax.random.fold_in(jax.random.fold_in(stream_key, 6), position), (parts,), jnp.float32, least / len(pieces), high / len(pieces))
        return jnp.repeat(jnp.exp(steps), shape[position] // parts).reshape((-1,) + (1,) * (len(shape) - position - 1))

    loudness = one(*pieces[0])
    for cut in pieces[1:]:
        loudness = loudness * one(*cut)
    return loudness


def noise(rng, shape, scale, reach, cuts=(), kind=jnp.bfloat16):
    drawn = jax.random.normal(rng, shape, jnp.float32) * scale
    if len(cuts) > 0:
        drawn = block_levels(rng, shape, cuts, -0.22, 0.18) * drawn
    return jnp.clip(drawn, min=-reach, max=reach).astype(kind)


def setup_inputs(seed: int = 0) -> dict:
    seeds = jax.random.split(jax.random.key(seed), 11)
    queries = draw_queries(jax.random.fold_in(seeds[10], 71), 0)
    prefix_keys = noise(seeds[1], (PREFIX, KVH * HD), 1.0, 6.0, ((0, 16),))
    prefix_values = noise(seeds[2], (PREFIX, KVH * HD), 1.0, 6.0, ((0, 16),))
    suffix_keys = noise(seeds[3], (ROWS, SUF, KVH * HD), 1.0, 6.0, ((0, 32), (1, 16)))
    suffix_values = noise(seeds[4], (ROWS, SUF, KVH * HD), 1.0, 6.0, ((0, 32), (1, 16)))
    new_keys = noise(seeds[5], (STEPS, ROWS, KVH * HD), 1.0, 6.0, ((1, 32),))
    new_values = noise(seeds[6], (STEPS, ROWS, KVH * HD), 1.0, 6.0, ((1, 32),))
    lengths = with_ends(jax.random.randint(seeds[7], (ROWS,), SUF // 16, SUF + 1), jax.random.fold_in(seeds[7], 1), SUF // 16, SUF).astype(jnp.int32)
    pair_of = draw_pair_of(jax.random.fold_in(seeds[10], 71), 0)
    guidance = jnp.clip(jax.random.uniform(seeds[9], (H,), jnp.float32, 1.0, 3.0), 1.0, 3.0)
    return dict(queries=queries, prefix_keys=prefix_keys, prefix_values=prefix_values, suffix_keys=suffix_keys, suffix_values=suffix_values, new_keys=new_keys, new_values=new_values, lengths=lengths, pair_of=pair_of, guidance=guidance)


def reference(queries, prefix_keys, prefix_values, suffix_keys, suffix_values, new_keys, new_values, lengths, pair_of, guidance):
    group = H // KVH
    scale = HD ** (-0.5)
    pre_keys = prefix_keys.astype(jnp.float32).reshape(PREFIX, KVH, HD)
    pre_values = prefix_values.astype(jnp.float32).reshape(PREFIX, KVH, HD)
    step_index = jnp.arange(STEPS, dtype=jnp.int32)

    def one_row(index):
        query = queries[:, index].astype(jnp.float32).reshape(STEPS, KVH, group, HD)
        keys = jnp.concatenate([pre_keys, suffix_keys[index].astype(jnp.float32).reshape(SUF, KVH, HD), new_keys[:, index].astype(jnp.float32).reshape(STEPS, KVH, HD)], 0)
        values = jnp.concatenate([pre_values, suffix_values[index].astype(jnp.float32).reshape(SUF, KVH, HD), new_values[:, index].astype(jnp.float32).reshape(STEPS, KVH, HD)], 0)
        live_suffix = jnp.arange(SUF, dtype=jnp.int32) < lengths[index]
        shared = jnp.concatenate([jnp.ones((PREFIX,), bool), live_suffix])
        shared = jnp.broadcast_to(shared[None, :], (STEPS, PREFIX + SUF))
        causal = step_index[None, :] <= step_index[:, None]
        live = jnp.concatenate([shared, causal], 1)
        scores = jnp.einsum('tkgd,nkd->tkgn', query, keys) * scale
        scores = jnp.where(live[:, None, None, :], scores, -1e+30)
        top = lax.optimization_barrier(jnp.max(scores, -1, keepdims=True))
        weights = jnp.exp(scores - top)
        total = lax.optimization_barrier(jnp.sum(weights, -1))
        rounded = lax.optimization_barrier(weights.astype(jnp.bfloat16)).astype(jnp.float32)
        summed = jnp.einsum('tkgn,nkd->tkgd', rounded, values)
        return (summed / total[..., None]).reshape(STEPS, H, HD).astype(jnp.bfloat16)
    attention = lax.map(one_row, jnp.arange(ROWS, dtype=jnp.int32))
    rows = jnp.arange(ROWS, dtype=jnp.int32)
    cond = attention[jnp.minimum(rows, pair_of)].astype(jnp.float32)
    uncond = attention[jnp.maximum(rows, pair_of)].astype(jnp.float32)
    mix = uncond + guidance[None, None, :, None] * (cond - uncond)
    norm = jnp.sqrt(lax.optimization_barrier(jnp.mean(mix * mix, -1, keepdims=True)) + 1e-06)
    guided = (mix / norm).astype(jnp.bfloat16)
    return jnp.transpose(guided, (1, 0, 2, 3)).reshape(STEPS, ROWS, H * HD)
```

```python
import functools

import jax
import jax.numpy as jnp
from jax import lax
from jax.experimental import pallas as pl
from jax.experimental.pallas import tpu as pltpu
from jax.sharding import PartitionSpec as P

HD = 128
LOG2E = 1.4426950408889634
LOW = -1e30
MESH = pl.DeviceIdType.MESH
F32 = jnp.float32
BF16 = jnp.bfloat16


def dot_nt(a, b):
    return lax.dot_general(a, b, (((1,), (1,)), ((), ())), preferred_element_type=F32)


def iota(shape, axis):
    return lax.broadcasted_iota(jnp.int32, shape, axis)


def kernel(
    seq,
    rows_axis,
    q_hbm,
    pk_hbm,
    pv_hbm,
    sk_hbm,
    sv_hbm,
    nk_hbm,
    nv_hbm,
    len_ref,
    pair_ref,
    guide_ref,
    out_ref,
    q_in,
    pk,
    pv,
    sk,
    sv,
    nk,
    nv,
    qb,
    qf,
    o_suf,
    m_suf,
    l_suf,
    send_o,
    send_s,
    recv_o,
    recv_s,
    att_own,
    att_far,
    in_sem,
    send_sem,
    recv_sem,
    att_sem,
):
    steps, row_dev, width = q_in.shape
    heads = width // HD
    kv_heads = pk.shape[1] // HD
    share = heads // seq
    group = heads // kv_heads
    per_kv = seq // kv_heads
    block = share * steps * row_dev
    half = block // 2
    kv_rows = group * steps * row_dev
    combos = group * steps
    suf_dev = sk.shape[1]
    tiles = pk.shape[0] // HD
    hops = seq // 2
    scale = HD**-0.5 * LOG2E

    me = lax.axis_index("seq")
    row = lax.axis_index("row")
    right, left = lax.rem(me + 1, seq), lax.rem(me + seq - 1, seq)
    across = lax.rem(row + rows_axis // 2, rows_axis)
    near = ((right, row), (left, row))

    loads = [
        pltpu.make_async_copy(src, dst, in_sem.at[i])
        for i, (src, dst) in enumerate(
            ((q_hbm, q_in), (sk_hbm, sk), (sv_hbm, sv), (pk_hbm, pk), (pv_hbm, pv), (nk_hbm, nk), (nv_hbm, nv))
        )
    ]
    for load in loads:
        load.start()

    barrier = pltpu.get_barrier_semaphore()
    for device in (*near, (me, across)):
        pl.semaphore_signal(barrier, inc=1, device_id=device, device_id_type=MESH)
    pl.semaphore_wait(barrier, 3)

    loads[0].wait()
    for head in range(heads):
        for t in range(steps):
            tile = q_in[t, :, head * HD : (head + 1) * HD]
            at = (head * steps + t) * row_dev
            qb[at : at + row_dev, :] = tile
            qf[at : at + row_dev, :] = tile.astype(F32)

    loads[1].wait()
    loads[2].wait()
    zeros = jnp.zeros((suf_dev, HD), BF16)
    ones = jnp.ones((suf_dev, HD), BF16)
    first_half = iota((combos, 2 * suf_dev), 1) < suf_dev
    spot = me * suf_dev + lax.rem(iota((combos, 2 * suf_dev), 1), suf_dev)

    def beside(a, b):
        top = jnp.concatenate([a, zeros], 1)
        low = jnp.concatenate([zeros, b], 1)
        return jnp.concatenate([top, low], 0)

    def suffix_row(r):
        live = spot < len_ref[r]
        for pair in range(kv_heads // 2):
            g0, g1 = 2 * pair, 2 * pair + 1
            at0 = pl.ds(g0 * kv_rows + r, combos, stride=row_dev)
            at1 = pl.ds(g1 * kv_rows + r, combos, stride=row_dev)
            q2 = jnp.concatenate([qf[at0, :], qf[at1, :]], 1).astype(BF16)
            k0 = sk[r, :, g0 * HD : (g0 + 1) * HD]
            k1 = sk[r, :, g1 * HD : (g1 + 1) * HD]
            s = dot_nt(q2, beside(k0, k1)) * scale
            s = jnp.where(live, s, LOW)
            m0 = jnp.max(jnp.where(first_half, s, LOW), 1, keepdims=True)
            m1 = jnp.max(jnp.where(first_half, LOW, s), 1, keepdims=True)
            w = jnp.exp2(s - jnp.where(first_half, m0, m1)).astype(BF16)
            v0 = sv[r, :, g0 * HD : (g0 + 1) * HD]
            v1 = sv[r, :, g1 * HD : (g1 + 1) * HD]
            values = jnp.concatenate([beside(v0, v1), beside(ones, ones)], 1)
            o = jnp.dot(w, values, preferred_element_type=F32)
            o_suf[at0, :] = o[:, :HD]
            o_suf[at1, :] = o[:, HD : 2 * HD]
            l_suf[at0, :] = o[:, 2 * HD : 3 * HD]
            l_suf[at1, :] = o[:, 3 * HD :]
            m_suf[at0, :] = jnp.broadcast_to(m0, (combos, HD))
            m_suf[at1, :] = jnp.broadcast_to(m1, (combos, HD))

    def suffix_rows(i, carry):
        for j in range(4):
            suffix_row(i * 4 + j)
        return carry

    lax.fori_loop(0, row_dev // 4, suffix_rows, 0)

    loads[3].wait()
    loads[4].wait()
    loads[5].wait()
    loads[6].wait()
    many_ones = jnp.ones((pk.shape[0], HD), BF16)

    def partial(dest):
        at = pl.ds(pl.multiple_of(dest * block, block), block)
        lanes = pl.ds(pl.multiple_of((dest // per_kv) * HD, HD), HD)
        s = dot_nt(qb[at, :], pk[:, lanes])
        m_low = m_suf[at, :]
        m = jnp.maximum(jnp.max(s, 1, keepdims=True) * scale, m_low)
        w = jnp.concatenate(
            [jnp.exp2(s[:, j * HD : (j + 1) * HD] * scale - m).astype(BF16) for j in range(tiles)], 1
        )
        values = jnp.concatenate([pv[:, lanes], many_ones], 1)
        o = jnp.dot(w, values, preferred_element_type=F32)
        f = jnp.exp2(m_low - m)
        total = o[:, HD:] + f * l_suf[at, :]
        return (o[:, :HD] + f * o_suf[at, :]) / total, m + jnp.log2(total)

    diagonal = iota((half, HD), 0) == iota((half, HD), 1)

    def flat(lse):
        return jnp.broadcast_to(jnp.sum(jnp.where(diagonal, lse, 0.0), 0, keepdims=True), (8, HD))

    def merge(o, stat, arrived_o, arrived_stat):
        gap = stat - arrived_stat
        weight = 1.0 / (1.0 + jnp.exp2(gap))
        column = jnp.sum(
            jnp.where(diagonal, jnp.broadcast_to(weight[:1], (half, HD)), 0.0), 1, keepdims=True
        )
        merged = o + column * (arrived_o.astype(F32) - o)
        return merged, jnp.maximum(stat, arrived_stat) + jnp.log2(1.0 + jnp.exp2(-jnp.abs(gap)))

    def copies(way, k, first, size):
        stat_at = pl.ds(first // half * 8, size // half * 8)
        return (
            pltpu.make_async_remote_copy(
                src_ref=send_o.at[way, k, pl.ds(first, size)],
                dst_ref=recv_o.at[way, k, pl.ds(first, size)],
                send_sem=send_sem.at[way, k, 0],
                recv_sem=recv_sem.at[way, k, 0],
                device_id=near[way],
                device_id_type=MESH,
            ),
            pltpu.make_async_remote_copy(
                src_ref=send_s.at[way, k, stat_at],
                dst_ref=recv_s.at[way, k, stat_at],
                send_sem=send_sem.at[way, k, 1],
                recv_sem=recv_sem.at[way, k, 1],
                device_id=near[way],
                device_id_type=MESH,
            ),
        )

    o, lse = partial(lax.rem(me + hops, seq))
    for way in range(2):
        part = slice(way * half, (way + 1) * half)
        send_o[way, 0, part, :] = o[part].astype(BF16)
        send_s[way, 0, way * 8 : way * 8 + 8, :] = flat(lse[part])
        for copy in copies(way, 0, way * half, half):
            copy.start()

    def hop(k, only):
        for way in range(2):
            dest = lax.rem(me + hops - k, seq) if way == 0 else lax.rem(me + seq - hops + k, seq)
            o, lse = partial(dest)
            stats = [flat(lse[:half]), flat(lse[half:])]
            if only:
                for copy in copies(way, 0, way * half, half):
                    copy.wait_recv()
            else:
                for copy in copies(way, k - 1, 0, block):
                    copy.wait_recv()
            for piece in range(2):
                part = slice(piece * half, (piece + 1) * half)
                stat_part = slice(piece * 8, piece * 8 + 8)
                o_piece, stat = o[part], stats[piece]
                if not only or piece == way:
                    o_piece, stat = merge(
                        o_piece, stat, recv_o[way, k - 1, part, :], recv_s[way, k - 1, stat_part, :]
                    )
                send_o[way, k, part, :] = o_piece.astype(BF16)
                send_s[way, k, stat_part, :] = stat
            for copy in copies(way, k, 0, block):
                copy.start()

    hop(1, True)

    def one_hop(k, carry):
        hop(k, False)
        return carry

    lax.fori_loop(2, hops, one_hop, 0)

    o, lse = partial(me)
    own_at = pl.multiple_of(me * block, block)
    lanes = pl.ds(pl.multiple_of((me // per_kv) * HD, HD), HD)
    new_k = [nk[j, :, lanes].astype(F32) for j in range(steps)]
    new_v = [nv[j, :, lanes].astype(F32) for j in range(steps)]
    own_o, own_lse = [], []
    for head in range(share):
        for t in range(steps):
            i = (head * steps + t) * row_dev
            query = qf[pl.ds(own_at + i, row_dev), :]
            fresh = [jnp.sum(query * new_k[j], 1, keepdims=True) * scale for j in range(t + 1)]
            base = lse[i : i + row_dev]
            top = base
            for score in fresh:
                top = jnp.maximum(top, score)
            weight = jnp.exp2(base - top)
            total, summed = weight, weight * o[i : i + row_dev]
            for j in range(t + 1):
                weight = jnp.exp2(fresh[j] - top)
                total = total + weight
                summed = summed + weight * new_v[j]
            own_o.append(summed / total)
            own_lse.append(top + jnp.log2(total))
    o = jnp.concatenate(own_o, 0)
    lse = jnp.concatenate(own_lse, 0)
    own = [(o[:half], flat(lse[:half])), (o[half:], flat(lse[half:]))]
    for way in range(2):
        for copy in copies(way, hops - 1, 0, block):
            copy.wait_recv()
        own = [
            merge(
                *own[piece],
                recv_o[way, hops - 1, piece * half : (piece + 1) * half, :],
                recv_s[way, hops - 1, piece * 8 : piece * 8 + 8, :],
            )
            for piece in range(2)
        ]
    for piece in range(2):
        att_own[piece * half : (piece + 1) * half, :] = own[piece][0].astype(BF16)

    swap = pltpu.make_async_remote_copy(
        src_ref=att_own,
        dst_ref=att_far,
        send_sem=att_sem.at[0],
        recv_sem=att_sem.at[1],
        device_id=(me, across),
        device_id_type=MESH,
    )
    swap.start()
    place = jnp.zeros((row_dev, row_dev), jnp.int32)
    for r in range(row_dev):
        partner = lax.rem(pair_ref[row * row_dev + r], row_dev)
        place = jnp.where(iota((row_dev, row_dev), 0) == r, partner, place)
    chosen = jnp.where(place == iota((row_dev, row_dev), 1), 1.0, 0.0).astype(BF16)
    is_low = jnp.broadcast_to(row, (row_dev, HD)) < rows_axis // 2
    swap.wait_recv()
    for head in range(share):
        guide = guide_ref[me * share + head]
        for t in range(steps):
            i = (head * steps + t) * row_dev
            mine = att_own[i : i + row_dev, :].astype(F32)
            other = jnp.dot(chosen, att_far[i : i + row_dev, :], preferred_element_type=F32)
            cond = jnp.where(is_low, mine, other)
            uncond = jnp.where(is_low, other, mine)
            mix = uncond + guide * (cond - uncond)
            norm = jnp.sqrt(jnp.mean(mix * mix, 1, keepdims=True) + 1e-06)
            out_ref[t, :, head * HD : (head + 1) * HD] = (mix / norm).astype(BF16)

    swap.wait_send()
    for way in range(2):
        for copy in copies(way, 0, way * half, half):
            copy.wait_send()

    def drain(k, carry):
        for way in range(2):
            for copy in copies(way, k, 0, block):
                copy.wait_send()
        return carry

    lax.fori_loop(1, hops, drain, 0)


def local(seq, rows_axis, queries, pk, pv, sk, sv, nk, nv, lengths, pair_of, guidance):
    steps, row_dev, width = queries.shape
    heads = width // HD
    share = heads // seq
    block = share * steps * row_dev
    hops = seq // 2
    whole = heads * steps * row_dev
    hbm = pl.BlockSpec(memory_space=pl.ANY)
    smem = pl.BlockSpec(memory_space=pltpu.SMEM)
    return pl.pallas_call(
        functools.partial(kernel, seq, rows_axis),
        out_shape=jax.ShapeDtypeStruct((steps, row_dev, share * HD), BF16),
        in_specs=[hbm] * 7 + [smem] * 3,
        out_specs=pl.BlockSpec(memory_space=pltpu.VMEM),
        scratch_shapes=[
            *(pltpu.VMEM(a.shape, a.dtype) for a in (queries, pk, pv, sk, sv, nk, nv)),
            pltpu.VMEM((whole, HD), BF16),
            pltpu.VMEM((whole, HD), F32),
            pltpu.VMEM((whole, HD), F32),
            pltpu.VMEM((whole, HD), F32),
            pltpu.VMEM((whole, HD), F32),
            pltpu.VMEM((2, hops, block, HD), BF16),
            pltpu.VMEM((2, hops, 16, HD), F32),
            pltpu.VMEM((2, hops, block, HD), BF16),
            pltpu.VMEM((2, hops, 16, HD), F32),
            pltpu.VMEM((block, HD), BF16),
            pltpu.VMEM((block, HD), BF16),
            pltpu.SemaphoreType.DMA((7,)),
            pltpu.SemaphoreType.DMA((2, hops, 2)),
            pltpu.SemaphoreType.DMA((2, hops, 2)),
            pltpu.SemaphoreType.DMA((2,)),
        ],
        compiler_params=pltpu.CompilerParams(
            collective_id=0, has_side_effects=True, vmem_limit_bytes=56 * 1024 * 1024
        ),
    )(queries, pk, pv, sk, sv, nk, nv, lengths, pair_of, guidance)


def solution(mesh):
    placed = (
        P(None, "row", None),
        P("seq", None),
        P("seq", None),
        P("row", "seq", None),
        P("row", "seq", None),
        P(None, "row", None),
        P(None, "row", None),
        P("row"),
        P(),
        P(),
    )
    body = functools.partial(local, mesh.shape["seq"], mesh.shape["row"])
    return jax.shard_map(
        body, mesh=mesh, in_specs=placed, out_specs=P(None, "row", "seq"), check_vma=False
    )
```

```python
import functools

import jax
import jax.numpy as jnp
from jax import lax
from jax.experimental import pallas as pl
from jax.experimental.pallas import tpu as pltpu
from jax.sharding import PartitionSpec as P

HD = 128
LOG2E = 1.4426950408889634
LOW = -1e30
MESH = pl.DeviceIdType.MESH
PARENT = {1: 0, 2: 0, 3: 2, 4: 2, 5: 4, 6: 4, 7: 6, 8: 6}
ORDER = (7, 6, 5, 4, 3, 2, 1)
MERGES = {4: (6,), 2: (4,), 1: (2,)}
F32 = jnp.float32
BF16 = jnp.bfloat16


def dot_nt(a, b):
    return lax.dot_general(a, b, (((1,), (1,)), ((), ())), preferred_element_type=F32)


def iota(shape, axis):
    return lax.broadcasted_iota(jnp.int32, shape, axis)


def kernel(
    seq,
    rows_axis,
    q_hbm,
    pk_hbm,
    pv_hbm,
    sk_hbm,
    sv_hbm,
    nk_hbm,
    nv_hbm,
    len_ref,
    pair_ref,
    guide_ref,
    out_ref,
    q_in,
    pk,
    pv,
    sk,
    sv,
    nk,
    nv,
    qb,
    qf,
    o_suf,
    m_suf,
    l_suf,
    send,
    recv,
    own_o,
    own_s,
    recv_far,
    own_msg,
    far_msg,
    in_sem,
    send_sem,
    recv_sem,
    send_far_sem,
    recv_far_sem,
    att_sem,
):
    steps, row_dev, width = q_in.shape
    heads = width // HD
    kv_heads = pk.shape[1] // HD
    share = heads // seq
    group = heads // kv_heads
    per_kv = seq // kv_heads
    block = share * steps * row_dev
    half = block // 2
    kv_rows = group * steps * row_dev
    combos = group * steps
    suf_dev = sk.shape[1]
    tiles = pk.shape[0] // HD
    hops = seq // 2
    scale = HD**-0.5 * LOG2E

    me = lax.axis_index("seq")
    row = lax.axis_index("row")
    across = lax.rem(row + rows_axis // 2, rows_axis)
    spans = sorted({d - p for d, p in PARENT.items()})

    last = [d for d in PARENT if PARENT[d] == 0]

    def reach(way, span, column):
        return (lax.rem(me + (span if way == 0 else seq - span), seq), column)

    loads = [
        pltpu.make_async_copy(src, dst, in_sem.at[i])
        for i, (src, dst) in enumerate(
            ((q_hbm, q_in), (sk_hbm, sk), (sv_hbm, sv), (pk_hbm, pk), (pv_hbm, pv), (nk_hbm, nk), (nv_hbm, nv))
        )
    ]
    for load in loads:
        load.start()

    barrier = pltpu.get_barrier_semaphore()
    peers = [reach(way, span, row) for span in spans for way in range(2)]
    peers += [reach(way, span, across) for span in last for way in range(2)] + [(me, across)]
    for device in peers:
        pl.semaphore_signal(barrier, inc=1, device_id=device, device_id_type=MESH)

    loads[0].wait()
    for head in range(heads):
        for t in range(steps):
            tile = q_in[t, :, head * HD : (head + 1) * HD]
            at = (head * steps + t) * row_dev
            qb[at : at + row_dev, :] = tile
            qf[at : at + row_dev, :] = tile.astype(F32)

    loads[1].wait()
    loads[2].wait()
    zeros = jnp.zeros((suf_dev, HD), BF16)
    ones = jnp.ones((suf_dev, HD), BF16)
    first_half = iota((combos, 2 * suf_dev), 1) < suf_dev
    spot = me * suf_dev + lax.rem(iota((combos, 2 * suf_dev), 1), suf_dev)

    def beside(a, b):
        top = jnp.concatenate([a, zeros], 1)
        low = jnp.concatenate([zeros, b], 1)
        return jnp.concatenate([top, low], 0)

    def suffix_row(r):
        live = spot < len_ref[r]
        for pair in range(kv_heads // 2):
            g0, g1 = 2 * pair, 2 * pair + 1
            at0 = pl.ds(g0 * kv_rows + r, combos, stride=row_dev)
            at1 = pl.ds(g1 * kv_rows + r, combos, stride=row_dev)
            q2 = jnp.concatenate([qf[at0, :], qf[at1, :]], 1).astype(BF16)
            k0 = sk[r, :, g0 * HD : (g0 + 1) * HD]
            k1 = sk[r, :, g1 * HD : (g1 + 1) * HD]
            s = dot_nt(q2, beside(k0, k1)) * scale
            s = jnp.where(live, s, LOW)
            m0 = jnp.max(jnp.where(first_half, s, LOW), 1, keepdims=True)
            m1 = jnp.max(jnp.where(first_half, LOW, s), 1, keepdims=True)
            w = jnp.exp2(s - jnp.where(first_half, m0, m1)).astype(BF16)
            v0 = sv[r, :, g0 * HD : (g0 + 1) * HD]
            v1 = sv[r, :, g1 * HD : (g1 + 1) * HD]
            values = jnp.concatenate([beside(v0, v1), beside(ones, ones)], 1)
            o = jnp.dot(w, values, preferred_element_type=F32)
            o_suf[at0, :] = o[:, :HD]
            o_suf[at1, :] = o[:, HD : 2 * HD]
            l_suf[at0, :] = o[:, 2 * HD : 3 * HD]
            l_suf[at1, :] = o[:, 3 * HD :]
            m_suf[at0, :] = jnp.broadcast_to(m0, (combos, HD))
            m_suf[at1, :] = jnp.broadcast_to(m1, (combos, HD))

    def suffix_rows(i, carry):
        for j in range(8):
            suffix_row(i * 8 + j)
        return carry

    lax.fori_loop(0, row_dev // 8, suffix_rows, 0)

    loads[3].wait()
    loads[4].wait()
    loads[5].wait()
    loads[6].wait()
    many_ones = jnp.ones((pk.shape[0], HD), BF16)

    def scores(dest):
        at = pl.ds(pl.multiple_of(dest * block, block), block)
        return dot_nt(qb[at, :], pk[:, pl.ds(pl.multiple_of((dest // per_kv) * HD, HD), HD)])

    def attend(dest, s):
        at = pl.ds(pl.multiple_of(dest * block, block), block)
        lanes = pl.ds(pl.multiple_of((dest // per_kv) * HD, HD), HD)
        m_low = m_suf[at, :]
        m = jnp.maximum(jnp.max(s, 1, keepdims=True) * scale, m_low)
        w = jnp.concatenate(
            [jnp.exp2(s[:, j * HD : (j + 1) * HD] * scale - m).astype(BF16) for j in range(tiles)], 1
        )
        values = jnp.concatenate([pv[:, lanes], many_ones], 1)
        o = jnp.dot(w, values, preferred_element_type=F32)
        f = jnp.exp2(m_low - m)
        total = o[:, HD:] + f * l_suf[at, :]
        return (o[:, :HD] + f * o_suf[at, :]) / total, m + jnp.log2(total)

    def partial(dest):
        return attend(dest, scores(dest))

    def partials(dests):
        s = [scores(dest) for dest in dests]
        return [attend(dest, one) for dest, one in zip(dests, s)]

    diagonal = iota((half, HD), 0) == iota((half, HD), 1)

    def flat(lse):
        return jnp.broadcast_to(jnp.sum(jnp.where(diagonal, lse, 0.0), 0, keepdims=True), (8, HD))

    row_in_tile = iota((8, HD), 0)

    def packed(stats):
        tiles = []
        for stat in stats:
            high = stat.astype(BF16).astype(F32)
            middle = (stat - high).astype(BF16).astype(F32)
            low = stat - high - middle
            tile = jnp.where(row_in_tile == 0, high, jnp.where(row_in_tile == 1, middle, low))
            tiles.append(jnp.where(row_in_tile < 3, tile, 0.0))
        return jnp.concatenate(tiles, 0).astype(BF16)

    def unpacked(rows, piece):
        tile = rows.astype(F32)[piece * 8 : piece * 8 + 8]
        return jnp.broadcast_to(jnp.sum(tile, 0, keepdims=True), (8, HD))

    def merge(o, stat, arrived_o, arrived_stat):
        gap = stat - arrived_stat
        weight = 1.0 / (1.0 + jnp.exp2(gap))
        column = jnp.sum(
            jnp.where(diagonal, jnp.broadcast_to(weight[:1], (half, HD)), 0.0), 1, keepdims=True
        )
        merged = o + column * (arrived_o.astype(F32) - o)
        return merged, jnp.maximum(stat, arrived_stat) + jnp.log2(1.0 + jnp.exp2(-jnp.abs(gap)))

    def message(way, d):
        size = 16 + (half if d == hops else block)
        return pltpu.make_async_remote_copy(
            src_ref=send.at[way, d - 1, pl.ds(0, size)],
            dst_ref=recv.at[way, d - 1, pl.ds(0, size)],
            send_sem=send_sem.at[way, d - 1],
            recv_sem=recv_sem.at[way, d - 1],
            device_id=reach(way, d - PARENT[d], row),
            device_id_type=MESH,
        )

    def message_across(way, d):
        return pltpu.make_async_remote_copy(
            src_ref=send.at[way, d - 1],
            dst_ref=recv_far.at[way, d - 1],
            send_sem=send_far_sem.at[way, d - 1],
            recv_sem=recv_far_sem.at[way, d - 1],
            device_id=reach(way, d, across),
            device_id_type=MESH,
        )

    def send_on(way, d):
        message(way, d).start()
        if PARENT[d] == 0:
            message_across(way, d).start()

    o, lse = partial(lax.rem(me + hops, seq))
    stats = packed([flat(lse[:half]), flat(lse[half:])])
    pl.semaphore_wait(barrier, len(peers))
    for way in range(2):
        send[way, hops - 1, :16, :] = stats
        send[way, hops - 1, 16 : 16 + half, :] = o[way * half : (way + 1) * half].astype(BF16)
        message(way, hops).start()

    children = {p: [d for d in PARENT if PARENT[d] == p] for p in range(hops)}

    def gather(way, d, pieces):
        for child in sorted(children[d]):
            message(way, child).wait_recv()
            stats = recv[way, child - 1, :16, :]
            for piece in range(2):
                if child == hops and piece != way:
                    continue
                at = 16 if child == hops else 16 + piece * half
                pieces[piece] = merge(
                    *pieces[piece], recv[way, child - 1, at : at + half, :], unpacked(stats, piece)
                )
        return pieces

    def pass_on(d):
        for way in range(2):
            pieces = [
                (
                    own_o[way, d - 1, piece * half : (piece + 1) * half, :],
                    own_s[way, d - 1, piece * 8 : piece * 8 + 8, :],
                )
                for piece in range(2)
            ]
            pieces = gather(way, d, pieces)
            send[way, d - 1, :16, :] = packed([stat for _, stat in pieces])
            for piece in range(2):
                at = 16 + piece * half
                send[way, d - 1, at : at + half, :] = pieces[piece][0].astype(BF16)
            send_on(way, d)

    def step(k, carry):
        d = jnp.int32(ORDER[0])
        for i in range(1, len(ORDER)):
            d = jnp.where(k == i, ORDER[i], d)
        dests = [lax.rem(me + (d if way == 0 else seq - d), seq) for way in range(2)]
        found = partials(dests)
        for way in range(2):
            o, lse = found[way]
            stats = [flat(lse[:half]), flat(lse[half:])]
            send[way, d - 1, :16, :] = packed(stats)
            send[way, d - 1, 16:, :] = o.astype(BF16)
            own_o[way, d - 1] = o
            own_s[way, d - 1] = jnp.concatenate(stats, 0)
        for way in range(2):
            for i in range(len(ORDER)):
                if not children[ORDER[i]]:
                    pl.when(k == i)(lambda way=way, i=i: send_on(way, ORDER[i]))
        for i in range(len(ORDER)):
            if MERGES.get(ORDER[i]):

                def merges(i=i):
                    for at in MERGES[ORDER[i]]:
                        pass_on(at)

                pl.when(k == i)(merges)
        return carry

    lax.fori_loop(0, len(ORDER), step, 0)

    o, lse = partial(me)
    own_at = pl.multiple_of(me * block, block)
    lanes = pl.ds(pl.multiple_of((me // per_kv) * HD, HD), HD)
    new_k = [nk[j, :, lanes].astype(F32) for j in range(steps)]
    new_v = [nv[j, :, lanes].astype(F32) for j in range(steps)]
    own_o, own_lse = [], []
    for head in range(share):
        for t in range(steps):
            i = (head * steps + t) * row_dev
            query = qf[pl.ds(own_at + i, row_dev), :]
            fresh = [jnp.sum(query * new_k[j], 1, keepdims=True) * scale for j in range(t + 1)]
            base = lse[i : i + row_dev]
            top = base
            for score in fresh:
                top = jnp.maximum(top, score)
            weight = jnp.exp2(base - top)
            total, summed = weight, weight * o[i : i + row_dev]
            for j in range(t + 1):
                weight = jnp.exp2(fresh[j] - top)
                total = total + weight
                summed = summed + weight * new_v[j]
            own_o.append(summed / total)
            own_lse.append(top + jnp.log2(total))
    o = jnp.concatenate(own_o, 0)
    lse = jnp.concatenate(own_lse, 0)
    own = [(o[:half], flat(lse[:half])), (o[half:], flat(lse[half:]))]
    own_msg[:16, :] = packed([stat for _, stat in own])
    own_msg[16:, :] = o.astype(BF16)
    swap = pltpu.make_async_remote_copy(
        src_ref=own_msg,
        dst_ref=far_msg,
        send_sem=att_sem.at[0],
        recv_sem=att_sem.at[1],
        device_id=(me, across),
        device_id_type=MESH,
    )
    swap.start()
    place = jnp.zeros((row_dev, row_dev), jnp.int32)
    for r in range(row_dev):
        partner = lax.rem(pair_ref[row * row_dev + r], row_dev)
        place = jnp.where(iota((row_dev, row_dev), 0) == r, partner, place)
    chosen = jnp.where(place == iota((row_dev, row_dev), 1), 1.0, 0.0).astype(BF16)
    is_low = jnp.broadcast_to(row, (row_dev, HD)) < rows_axis // 2

    def take(pieces, buffer, way, child):
        stats = buffer[way, child - 1, :16, :]
        return [
            merge(
                *pieces[piece],
                buffer[way, child - 1, 16 + piece * half : 16 + (piece + 1) * half, :],
                unpacked(stats, piece),
            )
            for piece in range(2)
        ]

    for child in last[:-1]:
        for way in range(2):
            message(way, child).wait_recv()
            own = take(own, recv, way, child)
    swap.wait_recv()
    stats = far_msg[:16, :]
    far = [
        (far_msg[16 + piece * half : 16 + (piece + 1) * half, :].astype(F32), unpacked(stats, piece))
        for piece in range(2)
    ]
    for child in last[:-1]:
        for way in range(2):
            message_across(way, child).wait_recv()
            far = take(far, recv_far, way, child)
    for way in range(2):
        message(way, last[-1]).wait_recv()
        own = take(own, recv, way, last[-1])
    for way in range(2):
        message_across(way, last[-1]).wait_recv()
        far = take(far, recv_far, way, last[-1])
    o = jnp.concatenate([own[0][0], own[1][0]], 0).astype(BF16)
    o_far = jnp.concatenate([far[0][0], far[1][0]], 0).astype(BF16)
    for head in range(share):
        guide = guide_ref[me * share + head]
        for t in range(steps):
            i = (head * steps + t) * row_dev
            mine = o[i : i + row_dev].astype(F32)
            other = jnp.dot(chosen, o_far[i : i + row_dev], preferred_element_type=F32)
            cond = jnp.where(is_low, mine, other)
            uncond = jnp.where(is_low, other, mine)
            mix = uncond + guide * (cond - uncond)
            norm = jnp.sqrt(jnp.mean(mix * mix, 1, keepdims=True) + 1e-06)
            out_ref[t, :, head * HD : (head + 1) * HD] = (mix / norm).astype(BF16)

    swap.wait_send()
    for way in range(2):
        for d in PARENT:
            message(way, d).wait_send()
        for d in last:
            message_across(way, d).wait_send()


def local(seq, rows_axis, queries, pk, pv, sk, sv, nk, nv, lengths, pair_of, guidance):
    steps, row_dev, width = queries.shape
    heads = width // HD
    share = heads // seq
    block = share * steps * row_dev
    hops = seq // 2
    whole = heads * steps * row_dev
    hbm = pl.BlockSpec(memory_space=pl.ANY)
    smem = pl.BlockSpec(memory_space=pltpu.SMEM)
    return pl.pallas_call(
        functools.partial(kernel, seq, rows_axis),
        out_shape=jax.ShapeDtypeStruct((steps, row_dev, share * HD), BF16),
        in_specs=[hbm] * 7 + [smem] * 3,
        out_specs=pl.BlockSpec(memory_space=pltpu.VMEM),
        scratch_shapes=[
            *(pltpu.VMEM(a.shape, a.dtype) for a in (queries, pk, pv, sk, sv, nk, nv)),
            pltpu.VMEM((whole, HD), BF16),
            pltpu.VMEM((whole, HD), F32),
            pltpu.VMEM((whole, HD), F32),
            pltpu.VMEM((whole, HD), F32),
            pltpu.VMEM((whole, HD), F32),
            pltpu.VMEM((2, hops, 16 + block, HD), BF16),
            pltpu.VMEM((2, hops, 16 + block, HD), BF16),
            pltpu.VMEM((2, hops - 1, block, HD), F32),
            pltpu.VMEM((2, hops - 1, 16, HD), F32),
            pltpu.VMEM((2, max(d for d in PARENT if PARENT[d] == 0), 16 + block, HD), BF16),
            pltpu.VMEM((16 + block, HD), BF16),
            pltpu.VMEM((16 + block, HD), BF16),
            pltpu.SemaphoreType.DMA((7,)),
            pltpu.SemaphoreType.DMA((2, hops)),
            pltpu.SemaphoreType.DMA((2, hops)),
            pltpu.SemaphoreType.DMA((2, hops)),
            pltpu.SemaphoreType.DMA((2, hops)),
            pltpu.SemaphoreType.DMA((2,)),
        ],
        compiler_params=pltpu.CompilerParams(
            collective_id=0, has_side_effects=True, vmem_limit_bytes=56 * 1024 * 1024
        ),
    )(queries, pk, pv, sk, sv, nk, nv, lengths, pair_of, guidance)


def solution(mesh):
    placed = (
        P(None, "row", None),
        P("seq", None),
        P("seq", None),
        P("row", "seq", None),
        P("row", "seq", None),
        P(None, "row", None),
        P(None, "row", None),
        P("row"),
        P(),
        P(),
    )
    body = functools.partial(local, mesh.shape["seq"], mesh.shape["row"])
    return jax.shard_map(
        body, mesh=mesh, in_specs=placed, out_specs=P(None, "row", "seq"), check_vma=False
    )
```

```python
import functools

import jax
import jax.numpy as jnp
from jax import lax
from jax.experimental import pallas as pl
from jax.experimental.pallas import tpu as pltpu
from jax.sharding import PartitionSpec as P

HD = 128
LOG2E = 1.4426950408889634
LOW = -1e30
MESH = pl.DeviceIdType.MESH
PARENT = {1: 0, 2: 0, 3: 2, 4: 2, 5: 4, 6: 4, 7: 6, 8: 6}
ORDER = (7, 6, 5, 4, 3, 2, 1)
EARLY = 4
MERGES = {5: (6,), 3: (4,), 1: (2,)}
F32 = jnp.float32
BF16 = jnp.bfloat16


def dot_nt(a, b):
    return lax.dot_general(a, b, (((1,), (1,)), ((), ())), preferred_element_type=F32)


def iota(shape, axis):
    return lax.broadcasted_iota(jnp.int32, shape, axis)


def kernel(
    seq,
    rows_axis,
    q_hbm,
    pk_hbm,
    pv_hbm,
    sk_hbm,
    sv_hbm,
    nk_hbm,
    nv_hbm,
    len_ref,
    pair_ref,
    guide_ref,
    out_ref,
    q_in,
    pk,
    pv,
    sk,
    sv,
    nk,
    nv,
    qb,
    qf,
    o_suf,
    m_suf,
    l_suf,
    send,
    recv,
    own_o,
    own_s,
    recv_far,
    own_msg,
    far_msg,
    att_own,
    att_far,
    in_sem,
    send_sem,
    recv_sem,
    send_far_sem,
    recv_far_sem,
    att_sem,
):
    steps, row_dev, width = q_in.shape
    heads = width // HD
    kv_heads = pk.shape[1] // HD
    share = heads // seq
    group = heads // kv_heads
    per_kv = seq // kv_heads
    block = share * steps * row_dev
    half = block // 2
    kv_rows = group * steps * row_dev
    combos = group * steps
    suf_dev = sk.shape[1]
    tiles = pk.shape[0] // HD
    hops = seq // 2
    scale = HD**-0.5 * LOG2E

    me = lax.axis_index("seq")
    row = lax.axis_index("row")
    across = lax.rem(row + rows_axis // 2, rows_axis)
    spans = sorted({d - p for d, p in PARENT.items()})

    last = [d for d in PARENT if PARENT[d] == 0]

    def reach(way, span, column):
        return (lax.rem(me + (span if way == 0 else seq - span), seq), column)

    loads = [
        pltpu.make_async_copy(src, dst, in_sem.at[i])
        for i, (src, dst) in enumerate(
            ((q_hbm, q_in), (sk_hbm, sk), (sv_hbm, sv), (pk_hbm, pk), (pv_hbm, pv), (nk_hbm, nk), (nv_hbm, nv))
        )
    ]
    for load in loads:
        load.start()

    barrier = pltpu.get_barrier_semaphore()
    peers = [reach(way, span, row) for span in spans for way in range(2)]
    peers += [reach(way, span, across) for span in last for way in range(2)] + [(me, across)]
    for device in peers:
        pl.semaphore_signal(barrier, inc=1, device_id=device, device_id_type=MESH)

    loads[0].wait()
    for head in range(heads):
        for t in range(steps):
            tile = q_in[t, :, head * HD : (head + 1) * HD]
            at = (head * steps + t) * row_dev
            qb[at : at + row_dev, :] = tile
            qf[at : at + row_dev, :] = tile.astype(F32)

    loads[1].wait()
    loads[2].wait()
    zeros = jnp.zeros((suf_dev, HD), BF16)
    ones = jnp.ones((suf_dev, HD), BF16)
    first_half = iota((combos, 2 * suf_dev), 1) < suf_dev
    spot = me * suf_dev + lax.rem(iota((combos, 2 * suf_dev), 1), suf_dev)

    def beside(a, b):
        top = jnp.concatenate([a, zeros], 1)
        low = jnp.concatenate([zeros, b], 1)
        return jnp.concatenate([top, low], 0)

    def suffix_row(r):
        live = spot < len_ref[r]
        for pair in range(kv_heads // 2):
            g0, g1 = 2 * pair, 2 * pair + 1
            at0 = pl.ds(g0 * kv_rows + r, combos, stride=row_dev)
            at1 = pl.ds(g1 * kv_rows + r, combos, stride=row_dev)
            q2 = jnp.concatenate([qf[at0, :], qf[at1, :]], 1).astype(BF16)
            k0 = sk[r, :, g0 * HD : (g0 + 1) * HD]
            k1 = sk[r, :, g1 * HD : (g1 + 1) * HD]
            s = dot_nt(q2, beside(k0, k1)) * scale
            s = jnp.where(live, s, LOW)
            m0 = jnp.max(jnp.where(first_half, s, LOW), 1, keepdims=True)
            m1 = jnp.max(jnp.where(first_half, LOW, s), 1, keepdims=True)
            w = jnp.exp2(s - jnp.where(first_half, m0, m1)).astype(BF16)
            v0 = sv[r, :, g0 * HD : (g0 + 1) * HD]
            v1 = sv[r, :, g1 * HD : (g1 + 1) * HD]
            values = jnp.concatenate([beside(v0, v1), beside(ones, ones)], 1)
            o = jnp.dot(w, values, preferred_element_type=F32)
            o_suf[at0, :] = o[:, :HD]
            o_suf[at1, :] = o[:, HD : 2 * HD]
            l_suf[at0, :] = o[:, 2 * HD : 3 * HD]
            l_suf[at1, :] = o[:, 3 * HD :]
            m_suf[at0, :] = jnp.broadcast_to(m0, (combos, HD))
            m_suf[at1, :] = jnp.broadcast_to(m1, (combos, HD))

    for r in range(row_dev):
        suffix_row(r)

    loads[3].wait()
    loads[4].wait()
    loads[5].wait()
    loads[6].wait()
    many_ones = jnp.ones((pk.shape[0], HD), BF16)

    def scores(dest):
        at = pl.ds(pl.multiple_of(dest * block, block), block)
        return dot_nt(qb[at, :], pk[:, pl.ds(pl.multiple_of((dest // per_kv) * HD, HD), HD)])

    def attend(dest, s):
        at = pl.ds(pl.multiple_of(dest * block, block), block)
        lanes = pl.ds(pl.multiple_of((dest // per_kv) * HD, HD), HD)
        m_low = m_suf[at, :]
        m = jnp.maximum(jnp.max(s, 1, keepdims=True) * scale, m_low)
        w = jnp.concatenate(
            [jnp.exp2(s[:, j * HD : (j + 1) * HD] * scale - m).astype(BF16) for j in range(tiles)], 1
        )
        values = jnp.concatenate([pv[:, lanes], many_ones], 1)
        o = jnp.dot(w, values, preferred_element_type=F32)
        f = jnp.exp2(m_low - m)
        total = o[:, HD:] + f * l_suf[at, :]
        return (o[:, :HD] + f * o_suf[at, :]) / total, m + jnp.log2(total)

    def partial(dest):
        return attend(dest, scores(dest))

    def partials(dests):
        s = [scores(dest) for dest in dests]
        return [attend(dest, one) for dest, one in zip(dests, s)]

    diagonal = iota((half, HD), 0) == iota((half, HD), 1)

    def flat(lse):
        return jnp.broadcast_to(jnp.sum(jnp.where(diagonal, lse, 0.0), 0, keepdims=True), (8, HD))

    row_in_tile = iota((8, HD), 0)

    def packed(stats):
        tiles = []
        for stat in stats:
            high = stat.astype(BF16).astype(F32)
            middle = (stat - high).astype(BF16).astype(F32)
            low = stat - high - middle
            tile = jnp.where(row_in_tile == 0, high, jnp.where(row_in_tile == 1, middle, low))
            tiles.append(jnp.where(row_in_tile < 3, tile, 0.0))
        return jnp.concatenate(tiles, 0).astype(BF16)

    def unpacked(rows, piece):
        tile = rows.astype(F32)[piece * 8 : piece * 8 + 8]
        return jnp.broadcast_to(jnp.sum(tile, 0, keepdims=True), (8, HD))

    def merge(o, stat, arrived_o, arrived_stat):
        gap = stat - arrived_stat
        weight = 1.0 / (1.0 + jnp.exp2(gap))
        column = jnp.sum(
            jnp.where(diagonal, jnp.broadcast_to(weight[:1], (half, HD)), 0.0), 1, keepdims=True
        )
        merged = o + column * (arrived_o.astype(F32) - o)
        return merged, jnp.maximum(stat, arrived_stat) + jnp.log2(1.0 + jnp.exp2(-jnp.abs(gap)))

    def message(way, d):
        size = 16 + (half if d == hops else block)
        return pltpu.make_async_remote_copy(
            src_ref=send.at[way, d - 1, pl.ds(0, size)],
            dst_ref=recv.at[way, d - 1, pl.ds(0, size)],
            send_sem=send_sem.at[way, d - 1],
            recv_sem=recv_sem.at[way, d - 1],
            device_id=reach(way, d - PARENT[d], row),
            device_id_type=MESH,
        )

    def message_across(way, d):
        return pltpu.make_async_remote_copy(
            src_ref=send.at[way, d - 1],
            dst_ref=recv_far.at[way, d - 1],
            send_sem=send_far_sem.at[way, d - 1],
            recv_sem=recv_far_sem.at[way, d - 1],
            device_id=reach(way, d, across),
            device_id_type=MESH,
        )

    def early(way, d):
        return lax.rem(me + (d if way == 0 else seq - d), seq) < EARLY

    def send_on(way, d):
        message(way, d).start()
        if PARENT[d] == 0:
            pl.when(early(way, d))(lambda: message_across(way, d).start())

    o, lse = partial(lax.rem(me + hops, seq))
    stats = packed([flat(lse[:half]), flat(lse[half:])])
    pl.semaphore_wait(barrier, len(peers))
    for way in range(2):
        send[way, hops - 1, :16, :] = stats
        send[way, hops - 1, 16 : 16 + half, :] = o[way * half : (way + 1) * half].astype(BF16)
        message(way, hops).start()

    children = {p: [d for d in PARENT if PARENT[d] == p] for p in range(hops)}

    def gather(way, d, pieces):
        for child in sorted(children[d]):
            message(way, child).wait_recv()
            stats = recv[way, child - 1, :16, :]
            for piece in range(2):
                if child == hops and piece != way:
                    continue
                at = 16 if child == hops else 16 + piece * half
                pieces[piece] = merge(
                    *pieces[piece], recv[way, child - 1, at : at + half, :], unpacked(stats, piece)
                )
        return pieces

    def pass_on(d):
        for way in range(2):
            pieces = [
                (
                    own_o[way, d - 1, piece * half : (piece + 1) * half, :],
                    own_s[way, d - 1, piece * 8 : piece * 8 + 8, :],
                )
                for piece in range(2)
            ]
            pieces = gather(way, d, pieces)
            send[way, d - 1, :16, :] = packed([stat for _, stat in pieces])
            for piece in range(2):
                at = 16 + piece * half
                send[way, d - 1, at : at + half, :] = pieces[piece][0].astype(BF16)
            send_on(way, d)

    def step(k, carry):
        d = jnp.int32(ORDER[0])
        for i in range(1, len(ORDER)):
            d = jnp.where(k == i, ORDER[i], d)
        dests = [lax.rem(me + (d if way == 0 else seq - d), seq) for way in range(2)]
        found = partials(dests)
        for way in range(2):
            o, lse = found[way]
            stats = [flat(lse[:half]), flat(lse[half:])]
            send[way, d - 1, :16, :] = packed(stats)
            send[way, d - 1, 16:, :] = o.astype(BF16)
            own_o[way, d - 1] = o
            own_s[way, d - 1] = jnp.concatenate(stats, 0)
        for way in range(2):
            for i in range(len(ORDER)):
                if not children[ORDER[i]]:
                    pl.when(k == i)(lambda way=way, i=i: send_on(way, ORDER[i]))
        for i in range(len(ORDER)):
            if MERGES.get(ORDER[i]):

                def merges(i=i):
                    for at in MERGES[ORDER[i]]:
                        pass_on(at)

                pl.when(k == i)(merges)
        return carry

    lax.fori_loop(0, len(ORDER), step, 0)

    o, lse = partial(me)
    own_at = pl.multiple_of(me * block, block)
    lanes = pl.ds(pl.multiple_of((me // per_kv) * HD, HD), HD)
    new_k = [nk[j, :, lanes].astype(F32) for j in range(steps)]
    new_v = [nv[j, :, lanes].astype(F32) for j in range(steps)]
    own_o, own_lse = [], []
    for head in range(share):
        for t in range(steps):
            i = (head * steps + t) * row_dev
            query = qf[pl.ds(own_at + i, row_dev), :]
            fresh = [jnp.sum(query * new_k[j], 1, keepdims=True) * scale for j in range(t + 1)]
            base = lse[i : i + row_dev]
            top = base
            for score in fresh:
                top = jnp.maximum(top, score)
            weight = jnp.exp2(base - top)
            total, summed = weight, weight * o[i : i + row_dev]
            for j in range(t + 1):
                weight = jnp.exp2(fresh[j] - top)
                total = total + weight
                summed = summed + weight * new_v[j]
            own_o.append(summed / total)
            own_lse.append(top + jnp.log2(total))
    o = jnp.concatenate(own_o, 0)
    lse = jnp.concatenate(own_lse, 0)
    own = [(o[:half], flat(lse[:half])), (o[half:], flat(lse[half:]))]
    def take(pieces, buffer, way, child):
        stats = buffer[way, child - 1, :16, :]
        return [
            merge(
                *pieces[piece],
                buffer[way, child - 1, 16 + piece * half : 16 + (piece + 1) * half, :],
                unpacked(stats, piece),
            )
            for piece in range(2)
        ]

    swap = pltpu.make_async_remote_copy(
        src_ref=own_msg,
        dst_ref=far_msg,
        send_sem=att_sem.at[0],
        recv_sem=att_sem.at[1],
        device_id=(me, across),
        device_id_type=MESH,
    )

    def att(pieces):
        return jnp.concatenate([pieces[0][0], pieces[1][0]], 0).astype(BF16)

    def finish_early():
        own_msg[:16, :] = packed([stat for _, stat in own])
        own_msg[16:, :] = o.astype(BF16)
        swap.start()
        mine = own
        for child in last[:-1]:
            for way in range(2):
                message(way, child).wait_recv()
                mine = take(mine, recv, way, child)
        swap.wait_recv()
        stats = far_msg[:16, :]
        far = [
            (far_msg[16 + piece * half : 16 + (piece + 1) * half, :].astype(F32), unpacked(stats, piece))
            for piece in range(2)
        ]
        for child in last[:-1]:
            for way in range(2):
                message_across(way, child).wait_recv()
                far = take(far, recv_far, way, child)
        for way in range(2):
            message(way, last[-1]).wait_recv()
            mine = take(mine, recv, way, last[-1])
        for way in range(2):
            message_across(way, last[-1]).wait_recv()
            far = take(far, recv_far, way, last[-1])
        att_own[...] = att(mine)
        att_far[...] = att(far)

    def finish_late():
        mine = own
        for child in last:
            for way in range(2):
                message(way, child).wait_recv()
                mine = take(mine, recv, way, child)
        own_msg[16:, :] = att(mine)
        own_msg[:16, :] = jnp.zeros((16, HD), BF16)
        swap.start()
        att_own[...] = own_msg[16:, :]
        swap.wait_recv()
        att_far[...] = far_msg[16:, :]

    place = jnp.zeros((row_dev, row_dev), jnp.int32)
    for r in range(row_dev):
        partner = lax.rem(pair_ref[row * row_dev + r], row_dev)
        place = jnp.where(iota((row_dev, row_dev), 0) == r, partner, place)
    chosen = jnp.where(place == iota((row_dev, row_dev), 1), 1.0, 0.0).astype(BF16)
    is_low = jnp.broadcast_to(row, (row_dev, HD)) < rows_axis // 2
    pl.when(me < EARLY)(finish_early)
    pl.when(me >= EARLY)(finish_late)
    for head in range(share):
        guide = guide_ref[me * share + head]
        for t in range(steps):
            i = (head * steps + t) * row_dev
            mine = att_own[i : i + row_dev, :].astype(F32)
            other = jnp.dot(chosen, att_far[i : i + row_dev, :], preferred_element_type=F32)
            cond = jnp.where(is_low, mine, other)
            uncond = jnp.where(is_low, other, mine)
            mix = uncond + guide * (cond - uncond)
            norm = jnp.sqrt(jnp.mean(mix * mix, 1, keepdims=True) + 1e-06)
            out_ref[t, :, head * HD : (head + 1) * HD] = (mix / norm).astype(BF16)

    swap.wait_send()
    for way in range(2):
        for d in PARENT:
            message(way, d).wait_send()
        for d in last:
            pl.when(early(way, d))(lambda way=way, d=d: message_across(way, d).wait_send())


def local(seq, rows_axis, queries, pk, pv, sk, sv, nk, nv, lengths, pair_of, guidance):
    steps, row_dev, width = queries.shape
    heads = width // HD
    share = heads // seq
    block = share * steps * row_dev
    hops = seq // 2
    whole = heads * steps * row_dev
    hbm = pl.BlockSpec(memory_space=pl.ANY)
    smem = pl.BlockSpec(memory_space=pltpu.SMEM)
    return pl.pallas_call(
        functools.partial(kernel, seq, rows_axis),
        out_shape=jax.ShapeDtypeStruct((steps, row_dev, share * HD), BF16),
        in_specs=[hbm] * 7 + [smem] * 3,
        out_specs=pl.BlockSpec(memory_space=pltpu.VMEM),
        scratch_shapes=[
            *(pltpu.VMEM(a.shape, a.dtype) for a in (queries, pk, pv, sk, sv, nk, nv)),
            pltpu.VMEM((whole, HD), BF16),
            pltpu.VMEM((whole, HD), F32),
            pltpu.VMEM((whole, HD), F32),
            pltpu.VMEM((whole, HD), F32),
            pltpu.VMEM((whole, HD), F32),
            pltpu.VMEM((2, hops, 16 + block, HD), BF16),
            pltpu.VMEM((2, hops, 16 + block, HD), BF16),
            pltpu.VMEM((2, hops - 1, block, HD), F32),
            pltpu.VMEM((2, hops - 1, 16, HD), F32),
            pltpu.VMEM((2, max(d for d in PARENT if PARENT[d] == 0), 16 + block, HD), BF16),
            pltpu.VMEM((16 + block, HD), BF16),
            pltpu.VMEM((16 + block, HD), BF16),
            pltpu.VMEM((block, HD), BF16),
            pltpu.VMEM((block, HD), BF16),
            pltpu.SemaphoreType.DMA((7,)),
            pltpu.SemaphoreType.DMA((2, hops)),
            pltpu.SemaphoreType.DMA((2, hops)),
            pltpu.SemaphoreType.DMA((2, hops)),
            pltpu.SemaphoreType.DMA((2, hops)),
            pltpu.SemaphoreType.DMA((2,)),
        ],
        compiler_params=pltpu.CompilerParams(
            collective_id=0, has_side_effects=True, vmem_limit_bytes=56 * 1024 * 1024
        ),
    )(queries, pk, pv, sk, sv, nk, nv, lengths, pair_of, guidance)


def solution(mesh):
    placed = (
        P(None, "row", None),
        P("seq", None),
        P("seq", None),
        P("row", "seq", None),
        P("row", "seq", None),
        P(None, "row", None),
        P(None, "row", None),
        P("row"),
        P(),
        P(),
    )
    body = functools.partial(local, mesh.shape["seq"], mesh.shape["row"])
    return jax.shard_map(
        body, mesh=mesh, in_specs=placed, out_specs=P(None, "row", "seq"), check_vma=False
    )
```

```python
import functools

import jax
import jax.numpy as jnp
from jax import lax
from jax.experimental import pallas as pl
from jax.experimental.pallas import tpu as pltpu
from jax.sharding import PartitionSpec as P

HD = 128
LOG2E = 1.4426950408889634
LOW = -1e30
MESH = pl.DeviceIdType.MESH
PARENT = {1: 0, 2: 0, 3: 2, 4: 2, 5: 4, 6: 4, 7: 6, 8: 6}
ORDER = (7, 6, 5, 4, 3, 2, 1)
EARLY = 4
MERGES = {5: (6,), 3: (4,), 1: (2,)}
F32 = jnp.float32
BF16 = jnp.bfloat16


def dot_nt(a, b):
    return lax.dot_general(a, b, (((1,), (1,)), ((), ())), preferred_element_type=F32)


def iota(shape, axis):
    return lax.broadcasted_iota(jnp.int32, shape, axis)


def kernel(
    seq,
    rows_axis,
    q_hbm,
    pk_hbm,
    pv_hbm,
    sk_hbm,
    sv_hbm,
    nk_hbm,
    nv_hbm,
    len_ref,
    pair_ref,
    guide_ref,
    out_ref,
    q_in,
    pk,
    pv,
    sk,
    sv,
    nk,
    nv,
    qb,
    qf,
    o_suf,
    m_suf,
    l_suf,
    send,
    recv,
    own_o,
    own_s,
    recv_far,
    own_msg,
    far_msg,
    att_own,
    att_far,
    in_sem,
    send_sem,
    recv_sem,
    send_far_sem,
    recv_far_sem,
    att_sem,
):
    steps, row_dev, width = q_in.shape
    heads = width // HD
    kv_heads = pk.shape[1] // HD
    share = heads // seq
    group = heads // kv_heads
    per_kv = seq // kv_heads
    block = share * steps * row_dev
    half = block // 2
    kv_rows = group * steps * row_dev
    combos = group * steps
    suf_dev = sk.shape[1]
    tiles = pk.shape[0] // HD
    hops = seq // 2
    scale = HD**-0.5 * LOG2E

    me = lax.axis_index("seq")
    row = lax.axis_index("row")
    across = lax.rem(row + rows_axis // 2, rows_axis)
    spans = sorted({d - p for d, p in PARENT.items()})

    last = [d for d in PARENT if PARENT[d] == 0]

    def reach(way, span, column):
        return (lax.rem(me + (span if way == 0 else seq - span), seq), column)

    loads = [
        pltpu.make_async_copy(src, dst, in_sem.at[i])
        for i, (src, dst) in enumerate(
            ((q_hbm, q_in), (sk_hbm, sk), (sv_hbm, sv), (pk_hbm, pk), (pv_hbm, pv), (nk_hbm, nk), (nv_hbm, nv))
        )
    ]
    for load in loads:
        load.start()

    barrier = pltpu.get_barrier_semaphore()
    peers = [reach(way, span, row) for span in spans for way in range(2)]
    peers += [reach(way, span, across) for span in last[-1:] for way in range(2)] + [(me, across)]
    for device in peers:
        pl.semaphore_signal(barrier, inc=1, device_id=device, device_id_type=MESH)

    loads[0].wait()
    for head in range(heads):
        for t in range(steps):
            tile = q_in[t, :, head * HD : (head + 1) * HD]
            at = (head * steps + t) * row_dev
            qb[at : at + row_dev, :] = tile
            qf[at : at + row_dev, :] = tile.astype(F32)

    loads[1].wait()
    loads[2].wait()
    zeros = jnp.zeros((suf_dev, HD), BF16)
    ones = jnp.ones((suf_dev, HD), BF16)
    first_half = iota((combos, 2 * suf_dev), 1) < suf_dev
    spot = me * suf_dev + lax.rem(iota((combos, 2 * suf_dev), 1), suf_dev)

    def beside(a, b):
        top = jnp.concatenate([a, zeros], 1)
        low = jnp.concatenate([zeros, b], 1)
        return jnp.concatenate([top, low], 0)

    def suffix_row(r):
        live = spot < len_ref[r]
        for pair in range(kv_heads // 2):
            g0, g1 = 2 * pair, 2 * pair + 1
            at0 = pl.ds(g0 * kv_rows + r, combos, stride=row_dev)
            at1 = pl.ds(g1 * kv_rows + r, combos, stride=row_dev)
            q2 = jnp.concatenate([qf[at0, :], qf[at1, :]], 1).astype(BF16)
            k0 = sk[r, :, g0 * HD : (g0 + 1) * HD]
            k1 = sk[r, :, g1 * HD : (g1 + 1) * HD]
            s = dot_nt(q2, beside(k0, k1)) * scale
            s = jnp.where(live, s, LOW)
            m0 = jnp.max(jnp.where(first_half, s, LOW), 1, keepdims=True)
            m1 = jnp.max(jnp.where(first_half, LOW, s), 1, keepdims=True)
            w = jnp.exp2(s - jnp.where(first_half, m0, m1)).astype(BF16)
            v0 = sv[r, :, g0 * HD : (g0 + 1) * HD]
            v1 = sv[r, :, g1 * HD : (g1 + 1) * HD]
            values = jnp.concatenate([beside(v0, v1), beside(ones, ones)], 1)
            o = jnp.dot(w, values, preferred_element_type=F32)
            o_suf[at0, :] = o[:, :HD]
            o_suf[at1, :] = o[:, HD : 2 * HD]
            l_suf[at0, :] = o[:, 2 * HD : 3 * HD]
            l_suf[at1, :] = o[:, 3 * HD :]
            m_suf[at0, :] = jnp.broadcast_to(m0, (combos, HD))
            m_suf[at1, :] = jnp.broadcast_to(m1, (combos, HD))

    for r in range(row_dev):
        suffix_row(r)

    loads[3].wait()
    loads[4].wait()
    loads[5].wait()
    loads[6].wait()
    many_ones = jnp.ones((pk.shape[0], HD), BF16)

    def scores(dest):
        at = pl.ds(pl.multiple_of(dest * block, block), block)
        return dot_nt(qb[at, :], pk[:, pl.ds(pl.multiple_of((dest // per_kv) * HD, HD), HD)])

    def attend(dest, s):
        at = pl.ds(pl.multiple_of(dest * block, block), block)
        lanes = pl.ds(pl.multiple_of((dest // per_kv) * HD, HD), HD)
        m_low = m_suf[at, :]
        m = jnp.maximum(jnp.max(s, 1, keepdims=True) * scale, m_low)
        w = jnp.concatenate(
            [jnp.exp2(s[:, j * HD : (j + 1) * HD] * scale - m).astype(BF16) for j in range(tiles)], 1
        )
        values = jnp.concatenate([pv[:, lanes], many_ones], 1)
        o = jnp.dot(w, values, preferred_element_type=F32)
        f = jnp.exp2(m_low - m)
        total = o[:, HD:] + f * l_suf[at, :]
        return (o[:, :HD] + f * o_suf[at, :]) / total, m + jnp.log2(total)

    def partial(dest):
        return attend(dest, scores(dest))

    def partials(dests):
        s = [scores(dest) for dest in dests]
        return [attend(dest, one) for dest, one in zip(dests, s)]

    diagonal = iota((half, HD), 0) == iota((half, HD), 1)

    def flat(lse):
        return jnp.broadcast_to(jnp.sum(jnp.where(diagonal, lse, 0.0), 0, keepdims=True), (8, HD))

    row_in_tile = iota((8, HD), 0)

    def packed(stats):
        tiles = []
        for stat in stats:
            high = stat.astype(BF16).astype(F32)
            middle = (stat - high).astype(BF16).astype(F32)
            low = stat - high - middle
            tile = jnp.where(row_in_tile == 0, high, jnp.where(row_in_tile == 1, middle, low))
            tiles.append(jnp.where(row_in_tile < 3, tile, 0.0))
        return jnp.concatenate(tiles, 0).astype(BF16)

    def unpacked(rows, piece):
        tile = rows.astype(F32)[piece * 8 : piece * 8 + 8]
        return jnp.broadcast_to(jnp.sum(tile, 0, keepdims=True), (8, HD))

    def merge(o, stat, arrived_o, arrived_stat):
        gap = stat - arrived_stat
        weight = 1.0 / (1.0 + jnp.exp2(gap))
        column = jnp.sum(
            jnp.where(diagonal, jnp.broadcast_to(weight[:1], (half, HD)), 0.0), 1, keepdims=True
        )
        merged = o + column * (arrived_o.astype(F32) - o)
        return merged, jnp.maximum(stat, arrived_stat) + jnp.log2(1.0 + jnp.exp2(-jnp.abs(gap)))

    def message(way, d):
        size = 16 + (half if d == hops else block)
        return pltpu.make_async_remote_copy(
            src_ref=send.at[way, d - 1, pl.ds(0, size)],
            dst_ref=recv.at[way, d - 1, pl.ds(0, size)],
            send_sem=send_sem.at[way, d - 1],
            recv_sem=recv_sem.at[way, d - 1],
            device_id=reach(way, d - PARENT[d], row),
            device_id_type=MESH,
        )

    def message_across(way, d):
        return pltpu.make_async_remote_copy(
            src_ref=send.at[way, d - 1],
            dst_ref=recv_far.at[way, d - 1],
            send_sem=send_far_sem.at[way, d - 1],
            recv_sem=recv_far_sem.at[way, d - 1],
            device_id=reach(way, d, across),
            device_id_type=MESH,
        )

    def early(way, d):
        return lax.rem(me + (d if way == 0 else seq - d), seq) < EARLY

    def send_on(way, d):
        message(way, d).start()
        if d == last[-1]:
            pl.when(early(way, d))(lambda: message_across(way, d).start())

    o, lse = partial(lax.rem(me + hops, seq))
    stats = packed([flat(lse[:half]), flat(lse[half:])])
    pl.semaphore_wait(barrier, len(peers))
    for way in range(2):
        send[way, hops - 1, :16, :] = stats
        send[way, hops - 1, 16 : 16 + half, :] = o[way * half : (way + 1) * half].astype(BF16)
        message(way, hops).start()

    children = {p: [d for d in PARENT if PARENT[d] == p] for p in range(hops)}

    def gather(way, d, pieces):
        for child in sorted(children[d]):
            message(way, child).wait_recv()
            stats = recv[way, child - 1, :16, :]
            for piece in range(2):
                if child == hops and piece != way:
                    continue
                at = 16 if child == hops else 16 + piece * half
                pieces[piece] = merge(
                    *pieces[piece], recv[way, child - 1, at : at + half, :], unpacked(stats, piece)
                )
        return pieces

    def pass_on(d):
        for way in range(2):
            pieces = [
                (
                    own_o[way, d - 1, piece * half : (piece + 1) * half, :],
                    own_s[way, d - 1, piece * 8 : piece * 8 + 8, :],
                )
                for piece in range(2)
            ]
            pieces = gather(way, d, pieces)
            send[way, d - 1, :16, :] = packed([stat for _, stat in pieces])
            for piece in range(2):
                at = 16 + piece * half
                send[way, d - 1, at : at + half, :] = pieces[piece][0].astype(BF16)
            send_on(way, d)

    def step(k, carry):
        d = jnp.int32(ORDER[0])
        for i in range(1, len(ORDER)):
            d = jnp.where(k == i, ORDER[i], d)
        dests = [lax.rem(me + (d if way == 0 else seq - d), seq) for way in range(2)]
        found = partials(dests)
        for way in range(2):
            o, lse = found[way]
            stats = [flat(lse[:half]), flat(lse[half:])]
            send[way, d - 1, :16, :] = packed(stats)
            send[way, d - 1, 16:, :] = o.astype(BF16)
            own_o[way, d - 1] = o
            own_s[way, d - 1] = jnp.concatenate(stats, 0)
        for way in range(2):
            for i in range(len(ORDER)):
                if not children[ORDER[i]]:
                    pl.when(k == i)(lambda way=way, i=i: send_on(way, ORDER[i]))
        for i in range(len(ORDER)):
            if MERGES.get(ORDER[i]):

                def merges(i=i):
                    for at in MERGES[ORDER[i]]:
                        pass_on(at)

                pl.when(k == i)(merges)
        return carry

    lax.fori_loop(0, len(ORDER), step, 0)

    o, lse = partial(me)
    own_at = pl.multiple_of(me * block, block)
    lanes = pl.ds(pl.multiple_of((me // per_kv) * HD, HD), HD)
    new_k = [nk[j, :, lanes].astype(F32) for j in range(steps)]
    new_v = [nv[j, :, lanes].astype(F32) for j in range(steps)]
    own_o, own_lse = [], []
    for head in range(share):
        for t in range(steps):
            i = (head * steps + t) * row_dev
            query = qf[pl.ds(own_at + i, row_dev), :]
            fresh = [jnp.sum(query * new_k[j], 1, keepdims=True) * scale for j in range(t + 1)]
            base = lse[i : i + row_dev]
            top = base
            for score in fresh:
                top = jnp.maximum(top, score)
            weight = jnp.exp2(base - top)
            total, summed = weight, weight * o[i : i + row_dev]
            for j in range(t + 1):
                weight = jnp.exp2(fresh[j] - top)
                total = total + weight
                summed = summed + weight * new_v[j]
            own_o.append(summed / total)
            own_lse.append(top + jnp.log2(total))
    o = jnp.concatenate(own_o, 0)
    lse = jnp.concatenate(own_lse, 0)
    own = [(o[:half], flat(lse[:half])), (o[half:], flat(lse[half:]))]
    def take(pieces, buffer, way, child):
        stats = buffer[way, child - 1, :16, :]
        return [
            merge(
                *pieces[piece],
                buffer[way, child - 1, 16 + piece * half : 16 + (piece + 1) * half, :],
                unpacked(stats, piece),
            )
            for piece in range(2)
        ]

    swap = pltpu.make_async_remote_copy(
        src_ref=own_msg,
        dst_ref=far_msg,
        send_sem=att_sem.at[0],
        recv_sem=att_sem.at[1],
        device_id=(me, across),
        device_id_type=MESH,
    )

    def att(pieces):
        return jnp.concatenate([pieces[0][0], pieces[1][0]], 0).astype(BF16)

    def finish_early():
        mine = own
        for child in last[:-1]:
            for way in range(2):
                message(way, child).wait_recv()
                mine = take(mine, recv, way, child)
        own_msg[:16, :] = packed([stat for _, stat in mine])
        own_msg[16:, :] = att(mine)
        swap.start()
        swap.wait_recv()
        stats = far_msg[:16, :]
        far = [
            (far_msg[16 + piece * half : 16 + (piece + 1) * half, :].astype(F32), unpacked(stats, piece))
            for piece in range(2)
        ]
        for way in range(2):
            message(way, last[-1]).wait_recv()
            mine = take(mine, recv, way, last[-1])
        for way in range(2):
            message_across(way, last[-1]).wait_recv()
            far = take(far, recv_far, way, last[-1])
        att_own[...] = att(mine)
        att_far[...] = att(far)

    def finish_late():
        mine = own
        for child in last:
            for way in range(2):
                message(way, child).wait_recv()
                mine = take(mine, recv, way, child)
        own_msg[16:, :] = att(mine)
        own_msg[:16, :] = jnp.zeros((16, HD), BF16)
        swap.start()
        att_own[...] = own_msg[16:, :]
        swap.wait_recv()
        att_far[...] = far_msg[16:, :]

    place = jnp.zeros((row_dev, row_dev), jnp.int32)
    for r in range(row_dev):
        partner = lax.rem(pair_ref[row * row_dev + r], row_dev)
        place = jnp.where(iota((row_dev, row_dev), 0) == r, partner, place)
    chosen = jnp.where(place == iota((row_dev, row_dev), 1), 1.0, 0.0).astype(BF16)
    is_low = jnp.broadcast_to(row, (row_dev, HD)) < rows_axis // 2
    pl.when(me < EARLY)(finish_early)
    pl.when(me >= EARLY)(finish_late)
    for head in range(share):
        guide = guide_ref[me * share + head]
        for t in range(steps):
            i = (head * steps + t) * row_dev
            mine = att_own[i : i + row_dev, :].astype(F32)
            other = jnp.dot(chosen, att_far[i : i + row_dev, :], preferred_element_type=F32)
            cond = jnp.where(is_low, mine, other)
            uncond = jnp.where(is_low, other, mine)
            mix = uncond + guide * (cond - uncond)
            norm = jnp.sqrt(jnp.mean(mix * mix, 1, keepdims=True) + 1e-06)
            out_ref[t, :, head * HD : (head + 1) * HD] = (mix / norm).astype(BF16)

    swap.wait_send()
    for way in range(2):
        for d in PARENT:
            message(way, d).wait_send()
        for d in last[-1:]:
            pl.when(early(way, d))(lambda way=way, d=d: message_across(way, d).wait_send())


def local(seq, rows_axis, queries, pk, pv, sk, sv, nk, nv, lengths, pair_of, guidance):
    steps, row_dev, width = queries.shape
    heads = width // HD
    share = heads // seq
    block = share * steps * row_dev
    hops = seq // 2
    whole = heads * steps * row_dev
    hbm = pl.BlockSpec(memory_space=pl.ANY)
    smem = pl.BlockSpec(memory_space=pltpu.SMEM)
    return pl.pallas_call(
        functools.partial(kernel, seq, rows_axis),
        out_shape=jax.ShapeDtypeStruct((steps, row_dev, share * HD), BF16),
        in_specs=[hbm] * 7 + [smem] * 3,
        out_specs=pl.BlockSpec(memory_space=pltpu.VMEM),
        scratch_shapes=[
            *(pltpu.VMEM(a.shape, a.dtype) for a in (queries, pk, pv, sk, sv, nk, nv)),
            pltpu.VMEM((whole, HD), BF16),
            pltpu.VMEM((whole, HD), F32),
            pltpu.VMEM((whole, HD), F32),
            pltpu.VMEM((whole, HD), F32),
            pltpu.VMEM((whole, HD), F32),
            pltpu.VMEM((2, hops, 16 + block, HD), BF16),
            pltpu.VMEM((2, hops, 16 + block, HD), BF16),
            pltpu.VMEM((2, hops - 1, block, HD), F32),
            pltpu.VMEM((2, hops - 1, 16, HD), F32),
            pltpu.VMEM((2, max(d for d in PARENT if PARENT[d] == 0), 16 + block, HD), BF16),
            pltpu.VMEM((16 + block, HD), BF16),
            pltpu.VMEM((16 + block, HD), BF16),
            pltpu.VMEM((block, HD), BF16),
            pltpu.VMEM((block, HD), BF16),
            pltpu.SemaphoreType.DMA((7,)),
            pltpu.SemaphoreType.DMA((2, hops)),
            pltpu.SemaphoreType.DMA((2, hops)),
            pltpu.SemaphoreType.DMA((2, hops)),
            pltpu.SemaphoreType.DMA((2, hops)),
            pltpu.SemaphoreType.DMA((2,)),
        ],
        compiler_params=pltpu.CompilerParams(
            collective_id=0, has_side_effects=True, vmem_limit_bytes=56 * 1024 * 1024
        ),
    )(queries, pk, pv, sk, sv, nk, nv, lengths, pair_of, guidance)


def solution(mesh):
    placed = (
        P(None, "row", None),
        P("seq", None),
        P("seq", None),
        P("row", "seq", None),
        P("row", "seq", None),
        P(None, "row", None),
        P(None, "row", None),
        P("row"),
        P(),
        P(),
    )
    body = functools.partial(local, mesh.shape["seq"], mesh.shape["row"])
    return jax.shard_map(
        body, mesh=mesh, in_specs=placed, out_specs=P(None, "row", "seq"), check_vma=False
    )
```

```python
import functools

import jax
import jax.numpy as jnp
from jax import lax
from jax.experimental import pallas as pl
from jax.experimental.pallas import tpu as pltpu
from jax.sharding import PartitionSpec as P

HD = 128
LOG2E = 1.4426950408889634
LOW = -1e30
MESH = pl.DeviceIdType.MESH
PARENT = {1: 0, 2: 0, 3: 2, 4: 2, 5: 4, 6: 4, 7: 6, 8: 6}
ORDER = (7, 6, 5, 4, 3, 2, 1)
EARLY = 4
MERGES = {5: (6,), 3: (4,), 1: (2,)}
F32 = jnp.float32
BF16 = jnp.bfloat16


def dot_nt(a, b):
    return lax.dot_general(a, b, (((1,), (1,)), ((), ())), preferred_element_type=F32)


def iota(shape, axis):
    return lax.broadcasted_iota(jnp.int32, shape, axis)


def kernel(
    seq,
    rows_axis,
    q_hbm,
    pk_hbm,
    pv_hbm,
    sk_hbm,
    sv_hbm,
    nk_hbm,
    nv_hbm,
    len_ref,
    pair_ref,
    guide_ref,
    out_ref,
    q_in,
    pk,
    pv,
    sk,
    sv,
    nk,
    nv,
    qb,
    qf,
    o_suf,
    m_suf,
    l_suf,
    send,
    recv,
    own_o,
    own_s,
    recv_far,
    own_msg,
    far_msg,
    att_own,
    att_far,
    in_sem,
    send_sem,
    recv_sem,
    send_far_sem,
    recv_far_sem,
    att_sem,
):
    steps, row_dev, width = q_in.shape
    heads = width // HD
    kv_heads = pk.shape[1] // HD
    share = heads // seq
    group = heads // kv_heads
    per_kv = seq // kv_heads
    block = share * steps * row_dev
    half = block // 2
    kv_rows = group * steps * row_dev
    combos = group * steps
    suf_dev = sk.shape[1]
    tiles = pk.shape[0] // HD
    hops = seq // 2
    scale = HD**-0.5 * LOG2E

    me = lax.axis_index("seq")
    row = lax.axis_index("row")
    across = lax.rem(row + rows_axis // 2, rows_axis)
    spans = sorted({d - p for d, p in PARENT.items()})

    last = [d for d in PARENT if PARENT[d] == 0]

    def reach(way, span, column):
        return (lax.rem(me + (span if way == 0 else seq - span), seq), column)

    loads = [
        pltpu.make_async_copy(src, dst, in_sem.at[i])
        for i, (src, dst) in enumerate(
            ((q_hbm, q_in), (sk_hbm, sk), (sv_hbm, sv), (pk_hbm, pk), (pv_hbm, pv), (nk_hbm, nk), (nv_hbm, nv))
        )
    ]
    for load in loads:
        load.start()

    barrier = pltpu.get_barrier_semaphore()
    peers = [reach(way, span, row) for span in spans for way in range(2)]
    peers += [reach(way, span, across) for span in last for way in range(2)] + [(me, across)]
    for device in peers:
        pl.semaphore_signal(barrier, inc=1, device_id=device, device_id_type=MESH)

    loads[0].wait()
    for head in range(heads):
        for t in range(steps):
            tile = q_in[t, :, head * HD : (head + 1) * HD]
            at = (head * steps + t) * row_dev
            qb[at : at + row_dev, :] = tile
            qf[at : at + row_dev, :] = tile.astype(F32)

    loads[1].wait()
    loads[2].wait()
    zeros = jnp.zeros((suf_dev, HD), BF16)
    ones = jnp.ones((suf_dev, HD), BF16)
    first_half = iota((combos, 2 * suf_dev), 1) < suf_dev
    spot = me * suf_dev + lax.rem(iota((combos, 2 * suf_dev), 1), suf_dev)

    def beside(a, b):
        top = jnp.concatenate([a, zeros], 1)
        low = jnp.concatenate([zeros, b], 1)
        return jnp.concatenate([top, low], 0)

    def suffix_row(r):
        live = spot < len_ref[r]
        for pair in range(kv_heads // 2):
            g0, g1 = 2 * pair, 2 * pair + 1
            at0 = pl.ds(g0 * kv_rows + r, combos, stride=row_dev)
            at1 = pl.ds(g1 * kv_rows + r, combos, stride=row_dev)
            q2 = jnp.concatenate([qf[at0, :], qf[at1, :]], 1).astype(BF16)
            k0 = sk[r, :, g0 * HD : (g0 + 1) * HD]
            k1 = sk[r, :, g1 * HD : (g1 + 1) * HD]
            s = dot_nt(q2, beside(k0, k1)) * scale
            s = jnp.where(live, s, LOW)
            m0 = jnp.max(jnp.where(first_half, s, LOW), 1, keepdims=True)
            m1 = jnp.max(jnp.where(first_half, LOW, s), 1, keepdims=True)
            w = jnp.exp2(s - jnp.where(first_half, m0, m1)).astype(BF16)
            v0 = sv[r, :, g0 * HD : (g0 + 1) * HD]
            v1 = sv[r, :, g1 * HD : (g1 + 1) * HD]
            values = jnp.concatenate([beside(v0, v1), beside(ones, ones)], 1)
            o = jnp.dot(w, values, preferred_element_type=F32)
            o_suf[at0, :] = o[:, :HD]
            o_suf[at1, :] = o[:, HD : 2 * HD]
            l_suf[at0, :] = o[:, 2 * HD : 3 * HD]
            l_suf[at1, :] = o[:, 3 * HD :]
            m_suf[at0, :] = jnp.broadcast_to(m0, (combos, HD))
            m_suf[at1, :] = jnp.broadcast_to(m1, (combos, HD))

    for r in range(row_dev):
        suffix_row(r)

    loads[3].wait()
    loads[4].wait()
    loads[5].wait()
    loads[6].wait()
    many_ones = jnp.ones((pk.shape[0], HD), BF16)

    def scores(dest):
        at = pl.ds(pl.multiple_of(dest * block, block), block)
        return dot_nt(qb[at, :], pk[:, pl.ds(pl.multiple_of((dest // per_kv) * HD, HD), HD)])

    def attend(dest, s):
        at = pl.ds(pl.multiple_of(dest * block, block), block)
        lanes = pl.ds(pl.multiple_of((dest // per_kv) * HD, HD), HD)
        m_low = m_suf[at, :]
        m = jnp.maximum(jnp.max(s, 1, keepdims=True) * scale, m_low)
        w = jnp.concatenate(
            [jnp.exp2(s[:, j * HD : (j + 1) * HD] * scale - m).astype(BF16) for j in range(tiles)], 1
        )
        values = jnp.concatenate([pv[:, lanes], many_ones], 1)
        o = jnp.dot(w, values, preferred_element_type=F32)
        f = jnp.exp2(m_low - m)
        total = o[:, HD:] + f * l_suf[at, :]
        return (o[:, :HD] + f * o_suf[at, :]) / total, m + jnp.log2(total)

    def partial(dest):
        return attend(dest, scores(dest))

    def partials(dests):
        s = [scores(dest) for dest in dests]
        return [attend(dest, one) for dest, one in zip(dests, s)]

    diagonal = iota((half, HD), 0) == iota((half, HD), 1)

    def flat(lse):
        return jnp.broadcast_to(jnp.sum(jnp.where(diagonal, lse, 0.0), 0, keepdims=True), (8, HD))

    row_in_tile = iota((8, HD), 0)

    def packed(stats):
        tiles = []
        for stat in stats:
            high = stat.astype(BF16).astype(F32)
            middle = (stat - high).astype(BF16).astype(F32)
            low = stat - high - middle
            tile = jnp.where(row_in_tile == 0, high, jnp.where(row_in_tile == 1, middle, low))
            tiles.append(jnp.where(row_in_tile < 3, tile, 0.0))
        return jnp.concatenate(tiles, 0).astype(BF16)

    def unpacked(rows, piece):
        tile = rows.astype(F32)[piece * 8 : piece * 8 + 8]
        return jnp.broadcast_to(jnp.sum(tile, 0, keepdims=True), (8, HD))

    def merge(o, stat, arrived_o, arrived_stat):
        gap = stat - arrived_stat
        weight = 1.0 / (1.0 + jnp.exp2(gap))
        column = jnp.sum(
            jnp.where(diagonal, jnp.broadcast_to(weight[:1], (half, HD)), 0.0), 1, keepdims=True
        )
        merged = o + column * (arrived_o.astype(F32) - o)
        return merged, jnp.maximum(stat, arrived_stat) + jnp.log2(1.0 + jnp.exp2(-jnp.abs(gap)))

    def message(way, d):
        size = 16 + (half if d == hops else block)
        return pltpu.make_async_remote_copy(
            src_ref=send.at[way, d - 1, pl.ds(0, size)],
            dst_ref=recv.at[way, d - 1, pl.ds(0, size)],
            send_sem=send_sem.at[way, d - 1],
            recv_sem=recv_sem.at[way, d - 1],
            device_id=reach(way, d - PARENT[d], row),
            device_id_type=MESH,
        )

    def message_across(way, d):
        return pltpu.make_async_remote_copy(
            src_ref=send.at[way, d - 1],
            dst_ref=recv_far.at[way, d - 1],
            send_sem=send_far_sem.at[way, d - 1],
            recv_sem=recv_far_sem.at[way, d - 1],
            device_id=reach(way, d, across),
            device_id_type=MESH,
        )

    def early(way, d):
        return lax.rem(me + (d if way == 0 else seq - d), seq) < EARLY

    def send_on(way, d):
        message(way, d).start()
        if PARENT[d] == 0:
            pl.when(early(way, d))(lambda: message_across(way, d).start())

    o, lse = partial(lax.rem(me + hops, seq))
    stats = packed([flat(lse[:half]), flat(lse[half:])])
    pl.semaphore_wait(barrier, len(peers))
    for way in range(2):
        send[way, hops - 1, :16, :] = stats
        send[way, hops - 1, 16 : 16 + half, :] = o[way * half : (way + 1) * half].astype(BF16)
        message(way, hops).start()

    children = {p: [d for d in PARENT if PARENT[d] == p] for p in range(hops)}

    def gather(way, d, pieces):
        for child in sorted(children[d]):
            message(way, child).wait_recv()
            stats = recv[way, child - 1, :16, :]
            for piece in range(2):
                if child == hops and piece != way:
                    continue
                at = 16 if child == hops else 16 + piece * half
                pieces[piece] = merge(
                    *pieces[piece], recv[way, child - 1, at : at + half, :], unpacked(stats, piece)
                )
        return pieces

    def pass_on(d):
        for way in range(2):
            pieces = [
                (
                    own_o[way, d - 1, piece * half : (piece + 1) * half, :],
                    own_s[way, d - 1, piece * 8 : piece * 8 + 8, :],
                )
                for piece in range(2)
            ]
            pieces = gather(way, d, pieces)
            send[way, d - 1, :16, :] = packed([stat for _, stat in pieces])
            for piece in range(2):
                at = 16 + piece * half
                send[way, d - 1, at : at + half, :] = pieces[piece][0].astype(BF16)
            send_on(way, d)

    def step(k, carry):
        d = jnp.int32(ORDER[0])
        for i in range(1, len(ORDER)):
            d = jnp.where(k == i, ORDER[i], d)
        dests = [lax.rem(me + (d if way == 0 else seq - d), seq) for way in range(2)]
        found = partials(dests)
        for way in range(2):
            o, lse = found[way]
            stats = [flat(lse[:half]), flat(lse[half:])]
            send[way, d - 1, :16, :] = packed(stats)
            send[way, d - 1, 16:, :] = o.astype(BF16)
            own_o[way, d - 1] = o
            own_s[way, d - 1] = jnp.concatenate(stats, 0)
        for way in range(2):
            for i in range(len(ORDER)):
                if not children[ORDER[i]]:
                    pl.when(k == i)(lambda way=way, i=i: send_on(way, ORDER[i]))
        for i in range(len(ORDER)):
            if MERGES.get(ORDER[i]):

                def merges(i=i):
                    for at in MERGES[ORDER[i]]:
                        pass_on(at)

                pl.when(k == i)(merges)
        return carry

    lax.fori_loop(0, len(ORDER), step, 0)

    o, lse = partial(me)
    own_at = pl.multiple_of(me * block, block)
    lanes = pl.ds(pl.multiple_of((me // per_kv) * HD, HD), HD)
    new_k = [nk[j, :, lanes].astype(F32) for j in range(steps)]
    new_v = [nv[j, :, lanes].astype(F32) for j in range(steps)]
    own_o, own_lse = [], []
    for head in range(share):
        for t in range(steps):
            i = (head * steps + t) * row_dev
            query = qf[pl.ds(own_at + i, row_dev), :]
            fresh = [jnp.sum(query * new_k[j], 1, keepdims=True) * scale for j in range(t + 1)]
            base = lse[i : i + row_dev]
            top = base
            for score in fresh:
                top = jnp.maximum(top, score)
            weight = jnp.exp2(base - top)
            total, summed = weight, weight * o[i : i + row_dev]
            for j in range(t + 1):
                weight = jnp.exp2(fresh[j] - top)
                total = total + weight
                summed = summed + weight * new_v[j]
            own_o.append(summed / total)
            own_lse.append(top + jnp.log2(total))
    o = jnp.concatenate(own_o, 0)
    lse = jnp.concatenate(own_lse, 0)
    own = [(o[:half], flat(lse[:half])), (o[half:], flat(lse[half:]))]
    def take(pieces, buffer, way, child):
        stats = buffer[way, child - 1, :16, :]
        return [
            merge(
                *pieces[piece],
                buffer[way, child - 1, 16 + piece * half : 16 + (piece + 1) * half, :],
                unpacked(stats, piece),
            )
            for piece in range(2)
        ]

    swap = pltpu.make_async_remote_copy(
        src_ref=own_msg,
        dst_ref=far_msg,
        send_sem=att_sem.at[0],
        recv_sem=att_sem.at[1],
        device_id=(me, across),
        device_id_type=MESH,
    )

    def att(pieces):
        return jnp.concatenate([pieces[0][0], pieces[1][0]], 0).astype(BF16)

    def finish_early():
        own_msg[:16, :] = packed([stat for _, stat in own])
        own_msg[16:, :] = o.astype(BF16)
        swap.start()
        mine = own
        for child in last[:-1]:
            for way in range(2):
                message(way, child).wait_recv()
                mine = take(mine, recv, way, child)
        swap.wait_recv()
        stats = far_msg[:16, :]
        far = [
            (far_msg[16 + piece * half : 16 + (piece + 1) * half, :].astype(F32), unpacked(stats, piece))
            for piece in range(2)
        ]
        for child in last[:-1]:
            for way in range(2):
                message_across(way, child).wait_recv()
                far = take(far, recv_far, way, child)
        for way in range(2):
            message(way, last[-1]).wait_recv()
            mine = take(mine, recv, way, last[-1])
        for way in range(2):
            message_across(way, last[-1]).wait_recv()
            far = take(far, recv_far, way, last[-1])
        att_own[...] = att(mine)
        att_far[...] = att(far)

    def finish_late():
        mine = own
        for child in last:
            for way in range(2):
                message(way, child).wait_recv()
                mine = take(mine, recv, way, child)
        own_msg[16:, :] = att(mine)
        own_msg[:16, :] = jnp.zeros((16, HD), BF16)
        swap.start()
        att_own[...] = own_msg[16:, :]
        swap.wait_recv()
        att_far[...] = far_msg[16:, :]

    place = jnp.zeros((row_dev, row_dev), jnp.int32)
    for r in range(row_dev):
        partner = lax.rem(pair_ref[row * row_dev + r], row_dev)
        place = jnp.where(iota((row_dev, row_dev), 0) == r, partner, place)
    chosen = jnp.where(place == iota((row_dev, row_dev), 1), 1.0, 0.0).astype(BF16)
    is_low = jnp.broadcast_to(row, (row_dev, HD)) < rows_axis // 2
    pl.when(me < EARLY)(finish_early)
    pl.when(me >= EARLY)(finish_late)
    for head in range(share):
        guide = guide_ref[me * share + head]
        for t in range(steps):
            i = (head * steps + t) * row_dev
            mine = att_own[i : i + row_dev, :].astype(F32)
            other = jnp.dot(chosen, att_far[i : i + row_dev, :], preferred_element_type=F32)
            cond = jnp.where(is_low, mine, other)
            uncond = jnp.where(is_low, other, mine)
            mix = uncond + guide * (cond - uncond)
            factor = lax.rsqrt(jnp.mean(mix * mix, 1, keepdims=True) + 1e-06)
            out_ref[t, :, head * HD : (head + 1) * HD] = (mix * factor).astype(BF16)

    swap.wait_send()
    for way in range(2):
        for d in PARENT:
            message(way, d).wait_send()
        for d in last:
            pl.when(early(way, d))(lambda way=way, d=d: message_across(way, d).wait_send())


def local(seq, rows_axis, queries, pk, pv, sk, sv, nk, nv, lengths, pair_of, guidance):
    steps, row_dev, width = queries.shape
    heads = width // HD
    share = heads // seq
    block = share * steps * row_dev
    hops = seq // 2
    whole = heads * steps * row_dev
    hbm = pl.BlockSpec(memory_space=pl.ANY)
    smem = pl.BlockSpec(memory_space=pltpu.SMEM)
    return pl.pallas_call(
        functools.partial(kernel, seq, rows_axis),
        out_shape=jax.ShapeDtypeStruct((steps, row_dev, share * HD), BF16),
        in_specs=[hbm] * 7 + [smem] * 3,
        out_specs=pl.BlockSpec(memory_space=pltpu.VMEM),
        scratch_shapes=[
            *(pltpu.VMEM(a.shape, a.dtype) for a in (queries, pk, pv, sk, sv, nk, nv)),
            pltpu.VMEM((whole, HD), BF16),
            pltpu.VMEM((whole, HD), F32),
            pltpu.VMEM((whole, HD), F32),
            pltpu.VMEM((whole, HD), F32),
            pltpu.VMEM((whole, HD), F32),
            pltpu.VMEM((2, hops, 16 + block, HD), BF16),
            pltpu.VMEM((2, hops, 16 + block, HD), BF16),
            pltpu.VMEM((2, hops - 1, block, HD), F32),
            pltpu.VMEM((2, hops - 1, 16, HD), F32),
            pltpu.VMEM((2, max(d for d in PARENT if PARENT[d] == 0), 16 + block, HD), BF16),
            pltpu.VMEM((16 + block, HD), BF16),
            pltpu.VMEM((16 + block, HD), BF16),
            pltpu.VMEM((block, HD), BF16),
            pltpu.VMEM((block, HD), BF16),
            pltpu.SemaphoreType.DMA((7,)),
            pltpu.SemaphoreType.DMA((2, hops)),
            pltpu.SemaphoreType.DMA((2, hops)),
            pltpu.SemaphoreType.DMA((2, hops)),
            pltpu.SemaphoreType.DMA((2, hops)),
            pltpu.SemaphoreType.DMA((2,)),
        ],
        compiler_params=pltpu.CompilerParams(
            collective_id=0, has_side_effects=True, vmem_limit_bytes=56 * 1024 * 1024
        ),
    )(queries, pk, pv, sk, sv, nk, nv, lengths, pair_of, guidance)


def solution(mesh):
    placed = (
        P(None, "row", None),
        P("seq", None),
        P("seq", None),
        P("row", "seq", None),
        P("row", "seq", None),
        P(None, "row", None),
        P(None, "row", None),
        P("row"),
        P(),
        P(),
    )
    body = functools.partial(local, mesh.shape["seq"], mesh.shape["row"])
    return jax.shard_map(
        body, mesh=mesh, in_specs=placed, out_specs=P(None, "row", "seq"), check_vma=False
    )
```
